32 devices in a mesh: groups: 2 (over x), domain: 16 (over z, y, core).
Axes of the slice: x: 2, y: 2, z: 4, core: 2. Of those that a mesh axis runs over, the one named last changes fastest.
Arguments:
- patches: bfloat16 [512, 125, 256], P(('groups', 'domain')), parts along dimension 0, may hold values from -6 to 6
- destination: int32 [512], P(('groups', 'domain')), parts along dimension 0, may hold values from 0 to 15, as said below
- cotangent: bfloat16 [1024, 4, 512], P(('groups', 'domain')), parts along dimension 0, may hold values from -16 to 16
- conv_weight: bfloat16 [256, 27, 64], replicated, may hold values from -0.21875 to 0.21875
- conv_bias: float32 [64], replicated, may hold values from -3 to 3
- head_weight: float32 [64, 4], replicated, may hold values from -0.75 to 0.75
Outputs:
- grad_conv: float32 [512, 27, 64], P(('groups', 'domain')), parts along dimension 0
- grad_bias: float32 [128], P('groups'), parts along dimension 0
- grad_head: float32 [128, 4], P('groups'), parts along dimension 0
The draws below stay inside these ranges and needn't reach their ends.
There are 2 independent parts, one for each index of `groups`. The reference program is written for one: setup_inputs(seed, part) draws one part's arguments, and reference() takes and returns one part's arrays. A program takes and returns all parts, laid end to end along the dimension named above; an argument that names none is the same for every part. Nothing has to cross between parts.
Inputs may be any that keep to these rules, and one draw needn't show every extreme that they name: `destination`: each trainer receives at most 32 patches and some trainer exactly 32; one owner sends at most 2 patch to one trainer and some pair reaches it; the patches of one trainer come from the owners as evenly as their number allows.
All inputs are finite; a program needn't handle non-finite values.
Results may differ from the reference program's by a relative error of at most 0.0029.
Values may be sent and summed in bfloat16 or wider, within the bound.
A program may use at most 64 MiB of HBM per device.

```python
import jax
import jax.numpy as jnp
from jax import lax

C_IN = 256
C_OUT = 64
FIELDS = 4
TAPS = 27
PS = 4
OWN = 16
PAD = 5
CELLS = 125
FINE = 512
OWNERS = 16
PATCHES = 256
TCAP = 32


def draw_destination(key, part):
    pair_key, spread_key, owner_key, shuffle_key = jax.random.split(key, 4)
    pair_order = jax.random.permutation(pair_key, OWNERS)
    half_count = OWNERS // 2
    spread_amount = jax.random.randint(spread_key, (half_count,), 0, OWN + 1).astype(jnp.int32)
    spread_amount = spread_amount.at[0].set(OWN)
    counts = jnp.zeros((OWNERS,), jnp.int32)
    counts = counts.at[pair_order[0::2]].set(OWN + spread_amount)
    counts = counts.at[pair_order[1::2]].set(OWN - spread_amount)
    count_ends = jnp.cumsum(counts)
    tickets = jnp.arange(PATCHES, dtype=jnp.int32)
    trainer_of = jnp.sum((count_ends[None, :] <= tickets[:, None]).astype(jnp.int32), axis=1)
    owner_order = jax.random.permutation(owner_key, OWNERS).astype(jnp.int32)
    owner_of = owner_order[tickets % OWNERS]
    slot_of = tickets // OWNERS
    shuffles = jax.vmap(lambda sub_key: jax.random.permutation(sub_key, OWN))(jax.random.split(shuffle_key, OWNERS))
    row_of = owner_of * OWN + shuffles[owner_of, slot_of].astype(jnp.int32)
    return jnp.zeros((PATCHES,), jnp.int32).at[row_of].set(trainer_of.astype(jnp.int32))


def spiked(drawn, key, source, target, parts, factor):
    def block_of(axis_at):
        return (jnp.arange(drawn.shape[axis_at]) // (drawn.shape[axis_at] // parts)).reshape((-1,) + (1,) * (drawn.ndim - 1 - axis_at))

    near = jax.random.permutation(key, parts)[block_of(target)]
    far = (block_of(target) + parts // 2) % parts
    return jnp.where((block_of(source) == near) | (block_of(source) == far), factor * drawn, drawn)


def steps_of(rng, shape, pieces, least, high):
    loudness, own = 1.0, jax.random.fold_in(rng, 6)
    for position, shards_of in pieces:
        draws = jnp.exp(jax.random.uniform(jax.random.fold_in(own, position), (shards_of,), jnp.float32, least / len(pieces), high / len(pieces)))
        loudness = loudness * jnp.repeat(draws, shape[position] // shards_of).reshape([-1 if axis == position else 1 for axis in range(len(shape))])
    return loudness


def scatter_about(stream_key, dims, scale, reach, shards=(), kind=jnp.bfloat16):
    factor_of = steps_of(stream_key, dims, shards, -0.22, 0.18) if shards else 1.0
    array = jax.random.normal(stream_key, dims, jnp.float32) * scale * factor_of
    return jnp.minimum(jnp.maximum(array, -reach), reach).astype(kind)


def noise_with(rng, extent, spread, reach, cuts, heavy, kind=jnp.bfloat16):
    drawn = spread * jax.random.normal(rng, extent, jnp.float32)
    if cuts:
        drawn = drawn * steps_of(rng, extent, cuts, -0.22, 0.18)
    return jnp.clip(spiked(drawn, jax.random.fold_in(rng, 3), *heavy), -reach, reach).astype(kind)


def setup_inputs(seed: int = 0, part: int = 0) -> dict:
    keys = jax.random.split(jax.random.key(seed), 7)
    part_keys = jax.random.split(jax.random.fold_in(keys[6], part), 7)
    return {
        "patches": noise_with(part_keys[0], (PATCHES, CELLS, C_IN), 1.0, 6.0, ((0, 16),), (0, 2, 16, 2.0)),
        "destination": draw_destination(jax.random.fold_in(jax.random.fold_in(keys[6], part), 71), part),
        "cotangent": scatter_about(part_keys[2], (OWNERS * TCAP, FIELDS, FINE), 4.0, 16.0, ((0, 16),)),
        "conv_weight": scatter_about(keys[3], (C_IN, TAPS, C_OUT), (C_IN * TAPS // 8) ** -0.5, 0.21875),
        "conv_bias": scatter_about(keys[4], (C_OUT,), 0.5, 3.0, (), jnp.float32),
        "head_weight": scatter_about(keys[5], (C_OUT, FIELDS), C_OUT ** -0.5, 0.75, (), jnp.float32),
    }


def trained_rows(destination):
    trainer_ids = jnp.arange(OWNERS, dtype=jnp.int32)
    dest_hits = (destination[:, None] == trainer_ids[None, :]).astype(jnp.int32)
    rank_list = jnp.sum(jnp.cumsum(dest_hits, axis=0) * dest_hits, axis=1) - 1
    return (destination * TCAP + rank_list).astype(jnp.int32)


def tap_split(tap_index):
    return tap_index // 9, (tap_index // 3) % 3, tap_index % 3


def forward_block(block_patches, conv_weight, conv_bias):
    block_count = block_patches.shape[0]
    flat_cells = block_patches.reshape(block_count * PAD ** 3, C_IN)
    grid_side = 2 * PS + 3
    canvas = jnp.zeros((block_count, grid_side, grid_side, grid_side, C_OUT), jnp.float32)
    for tap_index in range(TAPS):
        first_tap, second_tap, third_tap = tap_split(tap_index)
        product = jnp.dot(flat_cells, conv_weight[:, tap_index, :], preferred_element_type=jnp.float32)
        product = product.reshape(block_count, PAD, PAD, PAD, C_OUT)
        canvas = canvas.at[:, first_tap:first_tap + 2 * PAD:2, second_tap:second_tap + 2 * PAD:2,
                           third_tap:third_tap + 2 * PAD:2, :].add(product)
    return canvas[:, 1:1 + 2 * PS, 1:1 + 2 * PS, 1:1 + 2 * PS, :] + conv_bias


def weight_block(block_patches, grad_low):
    block_count = block_patches.shape[0]
    flat_cells = block_patches.reshape(block_count * PAD ** 3, C_IN)
    padded_grad = jnp.pad(grad_low, ((0, 0), (1, 2), (1, 2), (1, 2), (0, 0)))
    columns = []
    for tap_index in range(TAPS):
        first_tap, second_tap, third_tap = tap_split(tap_index)
        tap_view = padded_grad[:, first_tap:first_tap + 2 * PAD:2, second_tap:second_tap + 2 * PAD:2,
                               third_tap:third_tap + 2 * PAD:2, :].reshape(block_count * PAD ** 3, C_OUT)
        columns.append(jnp.dot(flat_cells.T, tap_view, preferred_element_type=jnp.float32))
    return jnp.stack(columns, axis=1)


def reference(patches, destination, cotangent, conv_weight, conv_bias, head_weight):
    cot_rows = trained_rows(destination)
    block_total = PATCHES // OWN
    patch_blocks = patches.reshape(block_total, OWN, PAD, PAD, PAD, C_IN)
    row_blocks = cot_rows.reshape(block_total, OWN)
    head_full = head_weight.astype(jnp.float32)

    def step_block(running, inputs):
        conv_sum, bias_sum, head_sum = running
        block_patches, block_rows = inputs
        hidden = forward_block(block_patches, conv_weight, conv_bias)
        cot_fine = cotangent[block_rows].astype(jnp.float32).reshape(OWN, FIELDS, 2 * PS, 2 * PS, 2 * PS)
        cot_fine = cot_fine.transpose(0, 2, 3, 4, 1)
        sigmoid_h = jax.nn.sigmoid(hidden)
        active = hidden * sigmoid_h
        upstream = jnp.einsum("bxyzf,of->bxyzo", cot_fine, head_full, precision=lax.Precision.HIGHEST)
        grad_hidden = upstream * sigmoid_h * (1.0 + hidden * (1.0 - sigmoid_h))
        grad_low = grad_hidden.astype(jnp.bfloat16)
        conv_sum = conv_sum + weight_block(block_patches, grad_low)
        bias_sum = bias_sum + jnp.sum(grad_hidden, axis=(0, 1, 2, 3))
        head_sum = head_sum + jnp.einsum("bxyzo,bxyzf->of", active, cot_fine, precision=lax.Precision.HIGHEST)
        return (conv_sum, bias_sum, head_sum), None

    initial = (jnp.zeros((C_IN, TAPS, C_OUT), jnp.float32), jnp.zeros((C_OUT,), jnp.float32),
               jnp.zeros((C_OUT, FIELDS), jnp.float32))
    totals, unused_out = lax.scan(step_block, initial, (patch_blocks, row_blocks))
    grad_scale = (PATCHES * PS ** 3) ** -0.5
    return totals[0] * grad_scale, totals[1] * grad_scale, totals[2] * grad_scale
```

```python
import functools
import itertools

import jax
import jax.numpy as jnp
import numpy as np
from jax import lax
from jax.experimental import pallas as pl
from jax.experimental.pallas import tpu as pltpu
from jax.sharding import PartitionSpec as P

FIELDS = 4
TAPS = 27
PS = 4
PAD = 5
CELLS = PAD**3
CELLS_UP = 128
COARSE = PS**3
FINE = 8 * COARSE
BITS = list(itertools.product((0, 1), repeat=3))


def tap_of(shift, parity):
    tap = 0
    for s, q in zip(BITS[shift], BITS[parity]):
        if s == 1 and q == 0:
            return None
        tap = 3 * tap + (1 if q == 0 else (0 if s == 1 else 2))
    return tap


@functools.cache
def pick_tables():
    cells = list(itertools.product(range(PS), repeat=3))
    shifts = np.zeros((8, 2, COARSE, 2, CELLS_UP), np.float32)
    fine = np.zeros((8, COARSE, FINE), np.float32)
    for b, (b1, b2, b3) in enumerate(BITS):
        for j, (j1, j2, j3) in enumerate(cells):
            cell = (j1 + b1) * PAD * PAD + (j2 + b2) * PAD + j3 + b3
            for half in range(2):
                shifts[b, half, j, half, cell] = 1
            fine[b, j, (2 * j1 + b1) * 4 * PS * PS + (2 * j2 + b2) * 2 * PS + 2 * j3 + b3] = 1
    shifts = shifts.reshape(16 * COARSE, 2 * CELLS_UP)
    return shifts, np.ascontiguousarray(shifts.T), fine.reshape(FINE, FINE)


def dot(a, b, dims=((1,), (0,))):
    return lax.dot_general(a, b, (dims, ((), ())), preferred_element_type=jnp.float32)


def layer_kernel(
    patch_ref, cot_ref, w_ref, bias_ref, head_ref, pick_ref, pick_t_ref, fine_ref,
    part_ref, small_ref,
    cells, wide, turned, grads, view, head_big, head_sum, bias_sum,
):
    slots = patch_ref.shape[0]
    c_in = patch_ref.shape[2]
    c_out = w_ref.shape[2]
    half = 4 * c_out
    group = slots * FIELDS
    quad = 4 * group
    bf = jnp.bfloat16

    cells[...] = jnp.zeros_like(cells)
    for p in range(slots):
        cells[p * CELLS_UP : p * CELLS_UP + CELLS, :] = patch_ref[p]
    wide[...] = jnp.zeros_like(wide)
    for s in range(8):
        for q in range(8):
            tap = tap_of(s, q)
            if tap is not None:
                wide[s * c_in : (s + 1) * c_in, q * c_out : (q + 1) * c_out] = w_ref[tap]

    moved = dot(fine_ref[...], cot_ref[...], ((1,), (1,))).astype(bf)
    for q in range(8):
        view[:, q * group : (q + 1) * group] = moved[q * COARSE : (q + 1) * COARSE]

    row = lax.broadcasted_iota(jnp.int32, (quad, half), 0)
    col = lax.broadcasted_iota(jnp.int32, (quad, half), 1)
    same = row // group == col // c_out
    spread = jnp.zeros((quad, half), jnp.float32)
    for f in range(FIELDS):
        spread = jnp.where(same & (row % FIELDS == f), head_ref[f : f + 1, :], spread)
    for t in range(3):
        term = spread.astype(bf)
        head_big[t * quad : (t + 1) * quad, :] = term
        spread = spread - term.astype(jnp.float32)

    head_sum[...] = jnp.zeros_like(head_sum)
    bias_sum[...] = jnp.zeros_like(bias_sum)
    lane_slot = lax.broadcasted_iota(jnp.int32, (2 * COARSE, 2 * quad), 1) % group // FIELDS
    row_slot = lax.broadcasted_iota(jnp.int32, (2 * COARSE, 2 * quad), 0) // COARSE

    @pl.loop(0, slots // 2)
    def _(pair):
        rows = pl.ds(pl.multiple_of(pair * 2 * COARSE, 2 * COARSE), 2 * COARSE)
        both = cells[pl.ds(pl.multiple_of(pair * 2 * CELLS_UP, 2 * CELLS_UP), 2 * CELLS_UP), :]
        shifted = dot(pick_ref[...], both).astype(bf)
        turn = dot(both, pick_t_ref[...], ((0,), (0,))).astype(bf)
        for s in range(8):
            turned[s, :, rows] = turn[:, s * 2 * COARSE : (s + 1) * 2 * COARSE]
        beside = jnp.concatenate(
            [shifted[s * 2 * COARSE : (s + 1) * 2 * COARSE] for s in range(8)], axis=1
        )
        here = view[...].astype(jnp.float32)
        here = jnp.concatenate([here, here], axis=0)
        here = jnp.where(lane_slot == row_slot + 2 * pair, here, 0.0).astype(bf)
        for h in range(2):
            lanes = slice(h * half, (h + 1) * half)
            deep = (4 + 4 * h) * c_in
            hidden = dot(beside[:, :deep], wide[:deep, lanes]) + bias_ref[:, lanes]
            mine = here[:, h * quad : (h + 1) * quad]
            upstream = dot(jnp.concatenate([mine] * 3, axis=1), head_big[...])
            gate = jax.nn.sigmoid(hidden)
            active = hidden * gate
            grad = upstream * gate * (1.0 + hidden * (1.0 - gate))
            grads[rows, lanes] = grad.astype(bf)
            bias_sum[:, lanes] += jnp.sum(grad, axis=0, keepdims=True)
            top = active.astype(bf)
            rest = (active - top.astype(jnp.float32)).astype(bf)
            head_sum[...] += dot(mine, jnp.concatenate([top, rest], axis=1), ((0,), (0,)))

    for s in range(8):
        for h in range(2):
            if s >= 4 and h == 0:
                continue
            block = dot(turned[s], grads[:, h * half : (h + 1) * half]).astype(bf)
            for r in range(4):
                tap = tap_of(s, 4 * h + r)
                if tap is not None:
                    part_ref[:, tap * c_out : (tap + 1) * c_out] = block[:, r * c_out : (r + 1) * c_out]

    small_ref[...] = jnp.zeros_like(small_ref)
    small_ref[0:1, :] = bias_sum[...]
    row = lax.broadcasted_iota(jnp.int32, (quad, 2 * half), 0)
    col = lax.broadcasted_iota(jnp.int32, (quad, 2 * half), 1)
    kept = jnp.where(row // group == col % half // c_out, head_sum[...], 0.0)
    for f in range(FIELDS):
        small_ref[4 + f : 5 + f, :] = jnp.sum(
            jnp.where(row % FIELDS == f, kept, 0.0), axis=0, keepdims=True
        )


def layer(patches, work_cot, conv_weight, conv_bias, head_weight):
    slots, _, c_in = patches.shape
    c_out = conv_weight.shape[2]
    group = slots * FIELDS
    tables = [jnp.asarray(table, jnp.bfloat16) for table in pick_tables()]
    return pl.pallas_call(
        layer_kernel,
        out_shape=(
            jax.ShapeDtypeStruct((c_in, TAPS * c_out), jnp.bfloat16),
            jax.ShapeDtypeStruct((8, 8 * c_out), jnp.float32),
        ),
        scratch_shapes=[
            pltpu.VMEM((slots * CELLS_UP, c_in), jnp.bfloat16),
            pltpu.VMEM((8 * c_in, 8 * c_out), jnp.bfloat16),
            pltpu.VMEM((8, c_in, slots * COARSE), jnp.bfloat16),
            pltpu.VMEM((slots * COARSE, 8 * c_out), jnp.bfloat16),
            pltpu.VMEM((COARSE, 8 * group), jnp.bfloat16),
            pltpu.VMEM((12 * group, 4 * c_out), jnp.bfloat16),
            pltpu.VMEM((4 * group, 8 * c_out), jnp.float32),
            pltpu.VMEM((1, 8 * c_out), jnp.float32),
        ],
        compiler_params=pltpu.CompilerParams(vmem_limit_bytes=48 * 1024 * 1024),
        cost_estimate=pl.CostEstimate(
            flops=8 * slots * COARSE * TAPS * c_in * c_out,
            bytes_accessed=6 * 1024 * 1024,
            transcendentals=slots * FINE * c_out,
        ),
    )(
        patches,
        work_cot.reshape(group, FINE),
        conv_weight.transpose(1, 0, 2),
        jnp.tile(conv_bias[None, :], (1, 8)),
        jnp.tile(head_weight.T, (1, 4)),
        *tables,
    )


def on_device(patches, destination, cotangent, conv_weight, conv_bias, head_weight):
    owners = lax.axis_size("domain")
    own_rows = patches.shape[0]
    train_rows = cotangent.shape[0]
    c_in, _, c_out = conv_weight.shape
    per_pair = (train_rows + owners - 1) // owners
    slot_total = owners * per_pair
    exchange = functools.partial(
        lax.all_to_all, axis_name="domain", split_axis=0, concat_axis=0, tiled=True
    )

    trainer_ids = jnp.arange(owners, dtype=jnp.int32)
    hits = (destination[:, None] == trainer_ids[None, :]).astype(jnp.int32)
    incoming = exchange(jnp.sum(hits, axis=0))
    earlier = jnp.arange(own_rows)[:, None] > jnp.arange(own_rows)[None, :]
    local_rank = jnp.sum(
        (earlier & (destination[:, None] == destination[None, :])).astype(jnp.int32), axis=1
    )
    before = trainer_ids[:, None] > trainer_ids[None, :]
    starts_in = jnp.sum(jnp.where(before, incoming[None, :], 0), axis=1)
    slot_rank = jnp.arange(per_pair, dtype=jnp.int32)
    slot_place = (starts_in[:, None] + slot_rank[None, :]).reshape(slot_total)
    outgoing = cotangent[jnp.minimum(slot_place, train_rows - 1)]
    arrived = exchange(outgoing.reshape(owners, per_pair, FIELDS, FINE))
    arrived = arrived.reshape(slot_total, FIELDS, FINE)
    work_cot = arrived[destination * per_pair + local_rank]

    part, small = layer(patches, work_cot, conv_weight, conv_bias, head_weight)

    scale = float((owners * own_rows * COARSE) ** (-0.5))
    small = jnp.sum(small.reshape(8, 8, c_out), axis=1)
    small = exchange(jnp.broadcast_to(small[None], (owners, 8, c_out)))
    small = jnp.sum(small, axis=0) * scale
    rows = c_in // owners
    terms = exchange(part.reshape(owners, rows, TAPS * c_out))
    conv = jnp.sum(terms.astype(jnp.float32), axis=0) * scale
    return conv.reshape(rows, TAPS, c_out), small[0], small[4:8].T


def solution(mesh):
    placed = (
        P(("groups", "domain"), None, None),
        P(("groups", "domain")),
        P(("groups", "domain"), None, None),
        P(),
        P(),
        P(),
    )
    return jax.shard_map(
        on_device,
        mesh=mesh,
        in_specs=placed,
        out_specs=(P(("groups", "domain"), None, None), P("groups"), P("groups", None)),
        check_vma=False,
    )
```

```python
import functools
import itertools

import jax
import jax.numpy as jnp
from jax import lax
from jax.experimental import pallas as pl
from jax.experimental.pallas import tpu as pltpu
from jax.sharding import PartitionSpec as P

FIELDS = 4
TAPS = 27
PS = 4
PAD = 5
CELLS = PAD**3
CELLS_UP = 128
COARSE = PS**3
FINE = 8 * COARSE
BITS = list(itertools.product((0, 1), repeat=3))


def tap_of(shift, parity):
    tap = 0
    for s, q in zip(BITS[shift], BITS[parity]):
        if s == 1 and q == 0:
            return None
        tap = 3 * tap + (1 if q == 0 else (0 if s == 1 else 2))
    return tap


def digits(index):
    return (index >> 4) & 3, (index >> 2) & 3, index & 3


def shifted_cell(index):
    j1, j2, j3 = digits(index & (COARSE - 1))
    shift = index >> 7
    cell = (j1 + (shift >> 2)) * PAD * PAD + (j2 + ((shift >> 1) & 1)) * PAD + j3 + (shift & 1)
    return ((index >> 6) & 1) * CELLS_UP + cell


def fine_cell(index):
    j1, j2, j3 = digits(index & (COARSE - 1))
    parity = index >> 6
    row = 2 * j1 + (parity >> 2)
    return (row * 2 * PS + 2 * j2 + ((parity >> 1) & 1)) * 2 * PS + 2 * j3 + (parity & 1)


def line(shape, axis):
    return lax.broadcasted_iota(jnp.int32, shape, axis)


def one_hot(mask):
    return jnp.where(mask, 1.0, 0.0).astype(jnp.bfloat16)


def dot(a, b, dims=((1,), (0,))):
    return lax.dot_general(a, b, (dims, ((), ())), preferred_element_type=jnp.float32)


def forward_kernel(
    patch_ref, w_ref, bias_ref, hidden_ref, turned_ref, cells, wide, pick, pick_t
):
    slots = patch_ref.shape[0]
    c_in = patch_ref.shape[2]
    c_out = w_ref.shape[2]
    half = 4 * c_out
    bf = jnp.bfloat16
    tall, short = 16 * COARSE, 2 * CELLS_UP

    pick[...] = one_hot(shifted_cell(line((tall, 1), 0)) == line((tall, short), 1))
    pick_t[...] = one_hot(shifted_cell(line((1, tall), 1)) == line((short, tall), 0))
    cells[...] = jnp.zeros_like(cells)
    for p in range(slots):
        cells[p * CELLS_UP : p * CELLS_UP + CELLS, :] = patch_ref[p]
    wide[...] = jnp.zeros_like(wide)
    for s in range(8):
        for q in range(8):
            tap = tap_of(s, q)
            if tap is not None:
                wide[s * c_in : (s + 1) * c_in, q * c_out : (q + 1) * c_out] = w_ref[tap]

    @pl.loop(0, slots // 2)
    def _(pair):
        rows = pl.ds(pl.multiple_of(pair * 2 * COARSE, 2 * COARSE), 2 * COARSE)
        both = cells[pl.ds(pl.multiple_of(pair * short, short), short), :]
        shifted = dot(pick[...], both).astype(bf)
        turn = dot(both, pick_t[...], ((0,), (0,))).astype(bf)
        for s in range(8):
            turned_ref[s, :, rows] = turn[:, s * 2 * COARSE : (s + 1) * 2 * COARSE]
        beside = jnp.concatenate(
            [shifted[s * 2 * COARSE : (s + 1) * 2 * COARSE] for s in range(8)], axis=1
        )
        for h in range(2):
            lanes = slice(h * half, (h + 1) * half)
            deep = (4 + 4 * h) * c_in
            hidden_ref[rows, lanes] = dot(beside[:, :deep], wide[:deep, lanes]) + bias_ref[:, lanes]


def backward_kernel(
    owner_rows, hidden_ref, turned_ref, cot_ref, head_ref, part_ref,
    grads, view, head_big, head_sum, bias_sum,
):
    slots = hidden_ref.shape[0] // COARSE
    half = hidden_ref.shape[1] // 2
    c_out = half // 4
    c_in = part_ref.shape[0]
    group = slots * FIELDS
    quad = 4 * group
    bf = jnp.bfloat16

    fine = one_hot(fine_cell(line((FINE, 1), 0)) == line((FINE, FINE), 1))
    moved = dot(fine, cot_ref[...], ((1,), (1,))).astype(bf)
    for q in range(8):
        view[:, q * group : (q + 1) * group] = moved[q * COARSE : (q + 1) * COARSE]

    row, col = line((quad, half), 0), line((quad, half), 1)
    same = row // group == col // c_out
    spread = jnp.zeros((quad, half), jnp.float32)
    for f in range(FIELDS):
        spread = jnp.where(same & (row % FIELDS == f), head_ref[f : f + 1, :], spread)
    for t in range(3):
        term = spread.astype(bf)
        head_big[t * quad : (t + 1) * quad, :] = term
        spread = spread - term.astype(jnp.float32)

    head_sum[...] = jnp.zeros_like(head_sum)
    bias_sum[...] = jnp.zeros_like(bias_sum)
    lane_slot = line((2 * COARSE, 2 * quad), 1) % group // FIELDS
    row_slot = line((2 * COARSE, 2 * quad), 0) // COARSE

    @pl.loop(0, slots // 2)
    def _(pair):
        rows = pl.ds(pl.multiple_of(pair * 2 * COARSE, 2 * COARSE), 2 * COARSE)
        here = view[...].astype(jnp.float32)
        here = jnp.concatenate([here, here], axis=0)
        here = jnp.where(lane_slot == row_slot + 2 * pair, here, 0.0).astype(bf)
        for h in range(2):
            lanes = slice(h * half, (h + 1) * half)
            hidden = hidden_ref[rows, lanes]
            mine = here[:, h * quad : (h + 1) * quad]
            upstream = dot(jnp.concatenate([mine] * 3, axis=1), head_big[...])
            gate = jax.nn.sigmoid(hidden)
            active = hidden * gate
            grad = upstream * gate * (1.0 + hidden * (1.0 - gate))
            grads[rows, lanes] = grad.astype(bf)
            bias_sum[:, lanes] += jnp.sum(grad, axis=0, keepdims=True)
            top = active.astype(bf)
            rest = (active - top.astype(jnp.float32)).astype(bf)
            head_sum[...] += dot(mine, jnp.concatenate([top, rest], axis=1), ((0,), (0,)))

    for s in range(8):
        for h in range(2):
            if s >= 4 and h == 0:
                continue
            block = dot(turned_ref[s], grads[:, h * half : (h + 1) * half]).astype(bf)
            for r in range(4):
                tap = tap_of(s, 4 * h + r)
                if tap is not None:
                    part_ref[:, tap * c_out : (tap + 1) * c_out] = block[:, r * c_out : (r + 1) * c_out]

    row, col = line((quad, 2 * half), 0), line((quad, 2 * half), 1)
    kept = jnp.where(row // group == col % half // c_out, head_sum[...], 0.0)
    sums = [bias_sum[...]]
    for f in range(FIELDS):
        sums.append(jnp.sum(jnp.where(row % FIELDS == f, kept, 0.0), axis=0, keepdims=True))
    sums = [sum(x[:, g * c_out : (g + 1) * c_out] for g in range(8)) for x in sums]
    tops = [x.astype(bf).astype(jnp.float32) for x in sums]
    tail = tops + [x - top for x, top in zip(sums, tops)]
    place = line((c_in, c_out), 0) % owner_rows
    for b in range(-(-len(tail) // owner_rows)):
        fill = jnp.zeros((c_in, c_out), jnp.float32)
        for i, value in enumerate(tail[b * owner_rows : (b + 1) * owner_rows]):
            fill = jnp.where(place == i, value, fill)
        part_ref[:, (TAPS + b) * c_out : (TAPS + b + 1) * c_out] = fill.astype(bf)


LIMIT = pltpu.CompilerParams(vmem_limit_bytes=32 * 1024 * 1024)


def forward(patches, conv_weight, conv_bias):
    slots, _, c_in = patches.shape
    c_out = conv_weight.shape[2]
    return pl.pallas_call(
        forward_kernel,
        out_shape=(
            jax.ShapeDtypeStruct((slots * COARSE, 8 * c_out), jnp.float32),
            jax.ShapeDtypeStruct((8, c_in, slots * COARSE), jnp.bfloat16),
        ),
        scratch_shapes=[
            pltpu.VMEM((slots * CELLS_UP, c_in), jnp.bfloat16),
            pltpu.VMEM((8 * c_in, 8 * c_out), jnp.bfloat16),
            pltpu.VMEM((16 * COARSE, 2 * CELLS_UP), jnp.bfloat16),
            pltpu.VMEM((2 * CELLS_UP, 16 * COARSE), jnp.bfloat16),
        ],
        compiler_params=LIMIT,
        cost_estimate=pl.CostEstimate(
            flops=8 * slots * COARSE * TAPS * c_in * c_out,
            bytes_accessed=10 * 1024 * 1024,
            transcendentals=0,
        ),
    )(patches, conv_weight.transpose(1, 0, 2), jnp.tile(conv_bias[None, :], (1, 8)))


def backward(hidden, turned, work_cot, head_weight, owner_rows):
    slots = work_cot.shape[0]
    c_in = turned.shape[1]
    c_out = head_weight.shape[0]
    group = slots * FIELDS
    blocks = TAPS + -(-2 * (FIELDS + 1) // owner_rows)
    return pl.pallas_call(
        functools.partial(backward_kernel, owner_rows),
        out_shape=jax.ShapeDtypeStruct((c_in, blocks * c_out), jnp.bfloat16),
        scratch_shapes=[
            pltpu.VMEM((slots * COARSE, 8 * c_out), jnp.bfloat16),
            pltpu.VMEM((COARSE, 8 * group), jnp.bfloat16),
            pltpu.VMEM((12 * group, 4 * c_out), jnp.bfloat16),
            pltpu.VMEM((4 * group, 8 * c_out), jnp.float32),
            pltpu.VMEM((1, 8 * c_out), jnp.float32),
        ],
        compiler_params=LIMIT,
        cost_estimate=pl.CostEstimate(
            flops=8 * slots * COARSE * TAPS * c_in * c_out,
            bytes_accessed=8 * 1024 * 1024,
            transcendentals=slots * FINE * c_out,
        ),
    )(hidden, turned, work_cot.reshape(group, FINE), jnp.tile(head_weight.T, (1, 4)))


def on_device(patches, destination, cotangent, conv_weight, conv_bias, head_weight):
    owners = lax.axis_size("domain")
    own_rows = patches.shape[0]
    train_rows = cotangent.shape[0]
    c_in, _, c_out = conv_weight.shape
    per_pair = (train_rows + owners - 1) // owners
    slot_total = owners * per_pair
    exchange = functools.partial(
        lax.all_to_all, axis_name="domain", split_axis=0, concat_axis=0, tiled=True
    )

    trainer_ids = jnp.arange(owners, dtype=jnp.int32)
    hits = (destination[:, None] == trainer_ids[None, :]).astype(jnp.int32)
    incoming = exchange(jnp.sum(hits, axis=0))
    earlier = jnp.arange(own_rows)[:, None] > jnp.arange(own_rows)[None, :]
    local_rank = jnp.sum(
        (earlier & (destination[:, None] == destination[None, :])).astype(jnp.int32), axis=1
    )
    before = trainer_ids[:, None] > trainer_ids[None, :]
    starts_in = jnp.sum(jnp.where(before, incoming[None, :], 0), axis=1)
    slot_rank = jnp.arange(per_pair, dtype=jnp.int32)
    slot_place = (starts_in[:, None] + slot_rank[None, :]).reshape(slot_total)
    outgoing = cotangent[jnp.minimum(slot_place, train_rows - 1)]
    patches, outgoing = lax.optimization_barrier((patches, outgoing))
    arrived = exchange(outgoing.reshape(owners, per_pair, FIELDS, FINE))
    hidden, turned = forward(patches, conv_weight, conv_bias)
    arrived = arrived.reshape(slot_total, FIELDS, FINE)
    work_cot = arrived[destination * per_pair + local_rank]

    rows = c_in // owners
    part = backward(hidden, turned, work_cot, head_weight, rows)
    terms = exchange(part.reshape(owners, rows, -1)).astype(jnp.float32)
    scale = float((owners * own_rows * COARSE) ** (-0.5))
    sums = jnp.sum(terms, axis=0) * scale
    conv = sums[:, : TAPS * c_out].reshape(rows, TAPS, c_out)
    tail = sums[:, TAPS * c_out :].reshape(rows, -1, c_out).transpose(1, 0, 2).reshape(-1, c_out)
    small = tail[: FIELDS + 1] + tail[FIELDS + 1 : 2 * (FIELDS + 1)]
    return conv, small[0], small[1:].T


def solution(mesh):
    placed = (
        P(("groups", "domain"), None, None),
        P(("groups", "domain")),
        P(("groups", "domain"), None, None),
        P(),
        P(),
        P(),
    )
    return jax.shard_map(
        on_device,
        mesh=mesh,
        in_specs=placed,
        out_specs=(P(("groups", "domain"), None, None), P("groups"), P("groups", None)),
        check_vma=False,
    )
```

```python
import functools
import itertools

import jax
import jax.numpy as jnp
from jax import lax
from jax.experimental import pallas as pl
from jax.experimental.pallas import tpu as pltpu
from jax.sharding import PartitionSpec as P

FIELDS = 4
TAPS = 27
PS = 4
PAD = 5
CELLS = PAD**3
CELLS_UP = 128
COARSE = PS**3
FINE = 8 * COARSE
BITS = list(itertools.product((0, 1), repeat=3))


def tap_of(shift, parity):
    tap = 0
    for s, q in zip(BITS[shift], BITS[parity]):
        if s == 1 and q == 0:
            return None
        tap = 3 * tap + (1 if q == 0 else (0 if s == 1 else 2))
    return tap


def digits(index):
    return (index >> 4) & 3, (index >> 2) & 3, index & 3


def shifted_cell(index):
    j1, j2, j3 = digits(index & (COARSE - 1))
    shift = index >> 7
    cell = (j1 + (shift >> 2)) * PAD * PAD + (j2 + ((shift >> 1) & 1)) * PAD + j3 + (shift & 1)
    return ((index >> 6) & 1) * CELLS_UP + cell


def fine_cell(index):
    j1, j2, j3 = digits(index & (COARSE - 1))
    parity = index >> 6
    row = 2 * j1 + (parity >> 2)
    return (row * 2 * PS + 2 * j2 + ((parity >> 1) & 1)) * 2 * PS + 2 * j3 + (parity & 1)


def line(shape, axis):
    return lax.broadcasted_iota(jnp.int32, shape, axis)


def one_hot(mask):
    return jnp.where(mask, 1.0, 0.0).astype(jnp.bfloat16)


def dot(a, b, dims=((1,), (0,))):
    return lax.dot_general(a, b, (dims, ((), ())), preferred_element_type=jnp.float32)


def forward_kernel(
    patch_ref, w_ref, bias_ref, hidden_ref, turned_ref, cells, wide, pick, pick_t
):
    slots = patch_ref.shape[0]
    c_in = patch_ref.shape[2]
    c_out = w_ref.shape[2]
    half = 4 * c_out
    bf = jnp.bfloat16
    tall, short = 16 * COARSE, 2 * CELLS_UP

    pick[...] = one_hot(shifted_cell(line((tall, 1), 0)) == line((tall, short), 1))
    pick_t[...] = one_hot(shifted_cell(line((1, tall), 1)) == line((short, tall), 0))
    cells[...] = jnp.zeros_like(cells)
    for p in range(slots):
        cells[p * CELLS_UP : p * CELLS_UP + CELLS, :] = patch_ref[p]
    wide[...] = jnp.zeros_like(wide)
    for s in range(8):
        for q in range(8):
            tap = tap_of(s, q)
            if tap is not None:
                wide[s * c_in : (s + 1) * c_in, q * c_out : (q + 1) * c_out] = w_ref[tap]

    @pl.loop(0, slots // 2)
    def _(pair):
        rows = pl.ds(pl.multiple_of(pair * 2 * COARSE, 2 * COARSE), 2 * COARSE)
        both = cells[pl.ds(pl.multiple_of(pair * short, short), short), :]
        shifted = dot(pick[...], both).astype(bf)
        turn = dot(both, pick_t[...], ((0,), (0,))).astype(bf)
        for s in range(8):
            turned_ref[s, :, rows] = turn[:, s * 2 * COARSE : (s + 1) * 2 * COARSE]
        beside = jnp.concatenate(
            [shifted[s * 2 * COARSE : (s + 1) * 2 * COARSE] for s in range(8)], axis=1
        )
        for h in range(2):
            lanes = slice(h * half, (h + 1) * half)
            deep = (4 + 4 * h) * c_in
            hidden_ref[rows, lanes] = dot(beside[:, :deep], wide[:deep, lanes]) + bias_ref[:, lanes]


def backward_kernel(
    owner_rows, hidden_ref, turned_ref, cot_ref, head_ref, part_ref,
    grads, view, head_big, head_sum, bias_sum,
):
    slots = hidden_ref.shape[0] // COARSE
    half = hidden_ref.shape[1] // 2
    c_out = half // 4
    c_in = part_ref.shape[0]
    group = slots * FIELDS
    quad = 4 * group
    bf = jnp.bfloat16

    fine = one_hot(fine_cell(line((FINE, 1), 0)) == line((FINE, FINE), 1))
    moved = dot(fine, cot_ref[...], ((1,), (1,))).astype(bf)
    for q in range(8):
        view[:, q * group : (q + 1) * group] = moved[q * COARSE : (q + 1) * COARSE]

    row, col = line((quad, half), 0), line((quad, half), 1)
    same = row // group == col // c_out
    spread = jnp.zeros((quad, half), jnp.float32)
    for f in range(FIELDS):
        spread = jnp.where(same & (row % FIELDS == f), head_ref[f : f + 1, :], spread)
    for t in range(3):
        term = spread.astype(bf)
        head_big[t * quad : (t + 1) * quad, :] = term
        spread = spread - term.astype(jnp.float32)

    head_sum[...] = jnp.zeros_like(head_sum)
    bias_sum[...] = jnp.zeros_like(bias_sum)
    lane_slot = line((2 * COARSE, 2 * quad), 1) % group // FIELDS
    row_slot = line((2 * COARSE, 2 * quad), 0) // COARSE

    @pl.loop(0, slots // 2)
    def _(pair):
        rows = pl.ds(pl.multiple_of(pair * 2 * COARSE, 2 * COARSE), 2 * COARSE)
        here = view[...].astype(jnp.float32)
        here = jnp.concatenate([here, here], axis=0)
        here = jnp.where(lane_slot == row_slot + 2 * pair, here, 0.0).astype(bf)
        for h in range(2):
            lanes = slice(h * half, (h + 1) * half)
            hidden = hidden_ref[rows, lanes]
            mine = here[:, h * quad : (h + 1) * quad]
            upstream = dot(jnp.concatenate([mine] * 3, axis=1), head_big[...])
            gate = jax.nn.sigmoid(hidden)
            active = hidden * gate
            grad = upstream * gate * (1.0 + hidden * (1.0 - gate))
            grads[rows, lanes] = grad.astype(bf)
            bias_sum[:, lanes] += jnp.sum(grad, axis=0, keepdims=True)
            top = active.astype(bf)
            rest = (active - top.astype(jnp.float32)).astype(bf)
            head_sum[...] += dot(mine, jnp.concatenate([top, rest], axis=1), ((0,), (0,)))

    for s in range(8):
        for h in range(2):
            if s >= 4 and h == 0:
                continue
            block = dot(turned_ref[s], grads[:, h * half : (h + 1) * half])
            for r in range(4):
                tap = tap_of(s, 4 * h + r)
                if tap is not None:
                    part_ref[:, tap * c_out : (tap + 1) * c_out] = block[:, r * c_out : (r + 1) * c_out]

    row, col = line((quad, 2 * half), 0), line((quad, 2 * half), 1)
    kept = jnp.where(row // group == col % half // c_out, head_sum[...], 0.0)
    sums = [bias_sum[...]]
    for f in range(FIELDS):
        sums.append(jnp.sum(jnp.where(row % FIELDS == f, kept, 0.0), axis=0, keepdims=True))
    tail = 2 * [sum(x[:, g * c_out : (g + 1) * c_out] for g in range(8)) for x in sums]
    place = line((c_in, c_out), 0) % owner_rows
    for b in range(-(-len(tail) // owner_rows)):
        fill = jnp.zeros((c_in, c_out), jnp.float32)
        for i, value in enumerate(tail[b * owner_rows : (b + 1) * owner_rows]):
            fill = jnp.where(place == i, value, fill)
        part_ref[:, (TAPS + b) * c_out : (TAPS + b + 1) * c_out] = fill


def reduce_kernel(
    c_out, scale, part_ref, out_ref, got, outgoing, landed, send_pair, recv_pair, send_far, recv_far
):
    peers, _, rows, width = part_ref.shape
    me = lax.axis_index("domain")
    side = lax.rem(me, 2)
    home = me // 2
    partner = me + 1 - 2 * side
    edge = TAPS * c_out

    barrier = pltpu.get_barrier_semaphore()
    pl.semaphore_signal(
        barrier, inc=1, device_id={"domain": partner}, device_id_type=pl.DeviceIdType.MESH
    )

    @pl.loop(1, peers)
    def _(step):
        pl.semaphore_signal(
            barrier,
            inc=1,
            device_id={"domain": 2 * lax.rem(home + step, peers) + side},
            device_id_type=pl.DeviceIdType.MESH,
        )

    pl.semaphore_wait(barrier, peers)

    def near(block):
        return pltpu.make_async_remote_copy(
            src_ref=part_ref.at[block, 1 - side],
            dst_ref=got.at[block],
            send_sem=send_pair.at[block],
            recv_sem=recv_pair.at[block],
            device_id={"domain": partner},
            device_id_type=pl.DeviceIdType.MESH,
        )

    def far(block, slot):
        return pltpu.make_async_remote_copy(
            src_ref=outgoing.at[block],
            dst_ref=landed.at[slot],
            send_sem=send_far.at[block],
            recv_sem=recv_far.at[slot],
            device_id={"domain": 2 * block + side},
            device_id_type=pl.DeviceIdType.MESH,
        )

    @pl.loop(1, peers + 1)
    def _(step):
        near(lax.rem(home + step, peers)).start()

    spot = line((rows, width), 0) + (line((rows, width), 1) - edge) // c_out * rows
    in_tail = line((rows, width), 1) >= edge
    low = in_tail & (spot >= FIELDS + 1)

    def pair_sum(block):
        near(block).wait_recv()
        both = part_ref[block, side] + got[block]
        top = both.astype(jnp.bfloat16).astype(jnp.float32)
        return jnp.where(low, both - top, jnp.where(in_tail, top, both))

    @pl.loop(1, peers)
    def _(step):
        block = lax.rem(home + step, peers)
        outgoing[block] = pair_sum(block).astype(jnp.bfloat16)
        far(block, home).start()

    out_ref[...] = pair_sum(home)

    @pl.loop(1, peers)
    def _(step):
        source = lax.rem(home + peers - step, peers)
        far(source, source).wait_recv()
        out_ref[...] += landed[source].astype(jnp.float32)

    out_ref[...] *= scale

    @pl.loop(1, peers)
    def _(step):
        block = lax.rem(home + step, peers)
        near(block).wait_send()
        far(block, home).wait_send()

    near(home).wait_send()


LIMIT = pltpu.CompilerParams(vmem_limit_bytes=22 * 1024 * 1024)


def add_up(part, c_out, owners, scale):
    rows, width = part.shape[0] // owners, part.shape[1]
    peers = owners // 2
    return pl.pallas_call(
        functools.partial(reduce_kernel, c_out, scale),
        out_shape=jax.ShapeDtypeStruct((rows, width), jnp.float32),
        in_specs=[pl.BlockSpec(memory_space=pltpu.VMEM)],
        out_specs=pl.BlockSpec(memory_space=pltpu.VMEM),
        scratch_shapes=[
            pltpu.VMEM((peers, rows, width), jnp.float32),
            pltpu.VMEM((peers, rows, width), jnp.bfloat16),
            pltpu.VMEM((peers, rows, width), jnp.bfloat16),
            pltpu.SemaphoreType.DMA((peers,)),
            pltpu.SemaphoreType.DMA((peers,)),
            pltpu.SemaphoreType.DMA((peers,)),
            pltpu.SemaphoreType.DMA((peers,)),
        ],
        compiler_params=pltpu.CompilerParams(
            collective_id=0, has_side_effects=True, vmem_limit_bytes=22 * 1024 * 1024
        ),
    )(part.reshape(peers, 2, rows, width))


def forward(patches, conv_weight, conv_bias):
    slots, _, c_in = patches.shape
    c_out = conv_weight.shape[2]
    return pl.pallas_call(
        forward_kernel,
        out_shape=(
            jax.ShapeDtypeStruct((slots * COARSE, 8 * c_out), jnp.float32),
            jax.ShapeDtypeStruct((8, c_in, slots * COARSE), jnp.bfloat16),
        ),
        scratch_shapes=[
            pltpu.VMEM((slots * CELLS_UP, c_in), jnp.bfloat16),
            pltpu.VMEM((8 * c_in, 8 * c_out), jnp.bfloat16),
            pltpu.VMEM((16 * COARSE, 2 * CELLS_UP), jnp.bfloat16),
            pltpu.VMEM((2 * CELLS_UP, 16 * COARSE), jnp.bfloat16),
        ],
        compiler_params=LIMIT,
        cost_estimate=pl.CostEstimate(
            flops=8 * slots * COARSE * TAPS * c_in * c_out,
            bytes_accessed=10 * 1024 * 1024,
            transcendentals=0,
        ),
    )(patches, conv_weight.transpose(1, 0, 2), jnp.tile(conv_bias[None, :], (1, 8)))


def backward(hidden, turned, work_cot, head_weight, owner_rows):
    slots = work_cot.shape[0]
    c_in = turned.shape[1]
    c_out = head_weight.shape[0]
    group = slots * FIELDS
    blocks = TAPS + -(-2 * (FIELDS + 1) // owner_rows)
    return pl.pallas_call(
        functools.partial(backward_kernel, owner_rows),
        out_shape=jax.ShapeDtypeStruct((c_in, blocks * c_out), jnp.float32),
        scratch_shapes=[
            pltpu.VMEM((slots * COARSE, 8 * c_out), jnp.bfloat16),
            pltpu.VMEM((COARSE, 8 * group), jnp.bfloat16),
            pltpu.VMEM((12 * group, 4 * c_out), jnp.bfloat16),
            pltpu.VMEM((4 * group, 8 * c_out), jnp.float32),
            pltpu.VMEM((1, 8 * c_out), jnp.float32),
        ],
        compiler_params=LIMIT,
        cost_estimate=pl.CostEstimate(
            flops=8 * slots * COARSE * TAPS * c_in * c_out,
            bytes_accessed=8 * 1024 * 1024,
            transcendentals=slots * FINE * c_out,
        ),
    )(hidden, turned, work_cot.reshape(group, FINE), jnp.tile(head_weight.T, (1, 4)))


def on_device(patches, destination, cotangent, conv_weight, conv_bias, head_weight):
    owners = lax.axis_size("domain")
    own_rows = patches.shape[0]
    train_rows = cotangent.shape[0]
    c_in, _, c_out = conv_weight.shape
    per_pair = (train_rows + owners - 1) // owners
    slot_total = owners * per_pair
    exchange = functools.partial(
        lax.all_to_all, axis_name="domain", split_axis=0, concat_axis=0, tiled=True
    )

    trainer_ids = jnp.arange(owners, dtype=jnp.int32)
    hits = (destination[:, None] == trainer_ids[None, :]).astype(jnp.int32)
    incoming = exchange(jnp.sum(hits, axis=0))
    earlier = jnp.arange(own_rows)[:, None] > jnp.arange(own_rows)[None, :]
    local_rank = jnp.sum(
        (earlier & (destination[:, None] == destination[None, :])).astype(jnp.int32), axis=1
    )
    before = trainer_ids[:, None] > trainer_ids[None, :]
    starts_in = jnp.sum(jnp.where(before, incoming[None, :], 0), axis=1)
    slot_rank = jnp.arange(per_pair, dtype=jnp.int32)
    slot_place = (starts_in[:, None] + slot_rank[None, :]).reshape(slot_total)
    outgoing = cotangent[jnp.minimum(slot_place, train_rows - 1)]
    patches, outgoing = lax.optimization_barrier((patches, outgoing))
    arrived = exchange(outgoing.reshape(owners, per_pair, FIELDS, FINE))
    hidden, turned = forward(patches, conv_weight, conv_bias)
    arrived = arrived.reshape(slot_total, FIELDS, FINE)
    work_cot = arrived[destination * per_pair + local_rank]

    rows = c_in // owners
    part = backward(hidden, turned, work_cot, head_weight, rows)
    scale = float((owners * own_rows * COARSE) ** (-0.5))
    sums = add_up(part, c_out, owners, scale)
    conv = sums[:, : TAPS * c_out].reshape(rows, TAPS, c_out)
    tail = sums[:, TAPS * c_out :].reshape(rows, -1, c_out).transpose(1, 0, 2).reshape(-1, c_out)
    small = tail[: FIELDS + 1] + tail[FIELDS + 1 : 2 * (FIELDS + 1)]
    return conv, small[0], small[1:].T


def solution(mesh):
    placed = (
        P(("groups", "domain"), None, None),
        P(("groups", "domain")),
        P(("groups", "domain"), None, None),
        P(),
        P(),
        P(),
    )
    return jax.shard_map(
        on_device,
        mesh=mesh,
        in_specs=placed,
        out_specs=(P(("groups", "domain"), None, None), P("groups"), P("groups", None)),
        check_vma=False,
    )
```

```python
import functools
import itertools

import jax
import jax.numpy as jnp
from jax import lax
from jax.experimental import pallas as pl
from jax.experimental.pallas import tpu as pltpu
from jax.sharding import PartitionSpec as P

FIELDS = 4
TAPS = 27
PS = 4
PAD = 5
CELLS = PAD**3
CELLS_UP = 128
COARSE = PS**3
FINE = 8 * COARSE
BITS = list(itertools.product((0, 1), repeat=3))


def tap_of(shift, parity):
    tap = 0
    for s, q in zip(BITS[shift], BITS[parity]):
        if s == 1 and q == 0:
            return None
        tap = 3 * tap + (1 if q == 0 else (0 if s == 1 else 2))
    return tap


def digits(index):
    return (index >> 4) & 3, (index >> 2) & 3, index & 3


def shifted_cell(index):
    j1, j2, j3 = digits(index & (COARSE - 1))
    shift = index >> 7
    cell = (j1 + (shift >> 2)) * PAD * PAD + (j2 + ((shift >> 1) & 1)) * PAD + j3 + (shift & 1)
    return ((index >> 6) & 1) * CELLS_UP + cell


def fine_cell(index):
    j1, j2, j3 = digits(index & (COARSE - 1))
    parity = index >> 6
    row = 2 * j1 + (parity >> 2)
    return (row * 2 * PS + 2 * j2 + ((parity >> 1) & 1)) * 2 * PS + 2 * j3 + (parity & 1)


def line(shape, axis):
    return lax.broadcasted_iota(jnp.int32, shape, axis)


def one_hot(mask):
    return jnp.where(mask, 1.0, 0.0).astype(jnp.bfloat16)


def dot(a, b, dims=((1,), (0,))):
    return lax.dot_general(a, b, (dims, ((), ())), preferred_element_type=jnp.float32)


def forward_kernel(
    patch_ref, w_ref, bias_ref, hidden_out, turned_out,
    hidden_ref, turned_ref, cells, wide, pick, pick_t, hidden_sem, turned_sem,
):
    slots = patch_ref.shape[0]
    c_in = patch_ref.shape[2]
    c_out = w_ref.shape[2]
    half = 4 * c_out
    bf = jnp.bfloat16
    tall, short = 16 * COARSE, 2 * CELLS_UP

    pick[...] = one_hot(shifted_cell(line((tall, 1), 0)) == line((tall, short), 1))
    pick_t[...] = one_hot(shifted_cell(line((1, tall), 1)) == line((short, tall), 0))
    cells[...] = jnp.zeros_like(cells)
    for p in range(slots):
        cells[p * CELLS_UP : p * CELLS_UP + CELLS, :] = patch_ref[p]
    wide[...] = jnp.zeros_like(wide)
    for s in range(8):
        for q in range(8):
            tap = tap_of(s, q)
            if tap is not None:
                wide[s * c_in : (s + 1) * c_in, q * c_out : (q + 1) * c_out] = w_ref[tap]

    def leave(pair):
        rows = pl.ds(pl.multiple_of(pair * 2 * COARSE, 2 * COARSE), 2 * COARSE)
        return (
            pltpu.make_async_copy(hidden_ref.at[rows, :], hidden_out.at[rows, :], hidden_sem.at[pair]),
            pltpu.make_async_copy(
                turned_ref.at[:, :, rows], turned_out.at[:, :, rows], turned_sem.at[pair]
            ),
        )

    @pl.loop(0, slots // 2)
    def _(pair):
        rows = pl.ds(pl.multiple_of(pair * 2 * COARSE, 2 * COARSE), 2 * COARSE)
        both = cells[pl.ds(pl.multiple_of(pair * short, short), short), :]
        shifted = dot(pick[...], both).astype(bf)
        turn = dot(both, pick_t[...], ((0,), (0,))).astype(bf)
        for s in range(8):
            turned_ref[s, :, rows] = turn[:, s * 2 * COARSE : (s + 1) * 2 * COARSE]
        beside = jnp.concatenate(
            [shifted[s * 2 * COARSE : (s + 1) * 2 * COARSE] for s in range(8)], axis=1
        )
        for h in range(2):
            lanes = slice(h * half, (h + 1) * half)
            deep = (4 + 4 * h) * c_in
            hidden_ref[rows, lanes] = dot(beside[:, :deep], wide[:deep, lanes]) + bias_ref[:, lanes]
        for copy in leave(pair):
            copy.start()

    @pl.loop(0, slots // 2)
    def _(pair):
        for copy in leave(pair):
            copy.wait()


def backward_kernel(
    owner_rows, hidden_in, turned_in, cot_ref, head_ref, part_ref,
    hidden_ref, turned_ref, grads, view, head_big, head_sum, bias_sum, hidden_sem, turned_sem,
):
    def fetch(pair):
        rows = pl.ds(pl.multiple_of(pair * 2 * COARSE, 2 * COARSE), 2 * COARSE)
        return pltpu.make_async_copy(
            hidden_in.at[rows, :], hidden_ref.at[rows, :], hidden_sem.at[pair]
        )

    @pl.loop(0, hidden_ref.shape[0] // (2 * COARSE))
    def _(pair):
        fetch(pair).start()

    fetch_turned = pltpu.make_async_copy(turned_in, turned_ref, turned_sem)
    fetch_turned.start()
    slots = hidden_ref.shape[0] // COARSE
    half = hidden_ref.shape[1] // 2
    c_out = half // 4
    c_in = part_ref.shape[0]
    group = slots * FIELDS
    quad = 4 * group
    bf = jnp.bfloat16

    fine = one_hot(fine_cell(line((FINE, 1), 0)) == line((FINE, FINE), 1))
    moved = dot(fine, cot_ref[...], ((1,), (1,))).astype(bf)
    for q in range(8):
        view[:, q * group : (q + 1) * group] = moved[q * COARSE : (q + 1) * COARSE]

    row, col = line((quad, half), 0), line((quad, half), 1)
    same = row // group == col // c_out
    spread = jnp.zeros((quad, half), jnp.float32)
    for f in range(FIELDS):
        spread = jnp.where(same & (row % FIELDS == f), head_ref[f : f + 1, :], spread)
    for t in range(3):
        term = spread.astype(bf)
        head_big[t * quad : (t + 1) * quad, :] = term
        spread = spread - term.astype(jnp.float32)

    head_sum[...] = jnp.zeros_like(head_sum)
    bias_sum[...] = jnp.zeros_like(bias_sum)
    lane_slot = line((2 * COARSE, 2 * quad), 1) % group // FIELDS
    row_slot = line((2 * COARSE, 2 * quad), 0) // COARSE

    @pl.loop(0, slots // 2)
    def _(pair):
        rows = pl.ds(pl.multiple_of(pair * 2 * COARSE, 2 * COARSE), 2 * COARSE)
        fetch(pair).wait()
        here = view[...].astype(jnp.float32)
        here = jnp.concatenate([here, here], axis=0)
        here = jnp.where(lane_slot == row_slot + 2 * pair, here, 0.0).astype(bf)
        for h in range(2):
            lanes = slice(h * half, (h + 1) * half)
            hidden = hidden_ref[rows, lanes]
            mine = here[:, h * quad : (h + 1) * quad]
            upstream = dot(jnp.concatenate([mine] * 3, axis=1), head_big[...])
            gate = jax.nn.sigmoid(hidden)
            active = hidden * gate
            grad = upstream * gate * (1.0 + hidden * (1.0 - gate))
            grads[rows, lanes] = grad.astype(bf)
            bias_sum[:, lanes] += jnp.sum(grad, axis=0, keepdims=True)
            top = active.astype(bf)
            rest = (active - top.astype(jnp.float32)).astype(bf)
            head_sum[...] += dot(mine, jnp.concatenate([top, rest], axis=1), ((0,), (0,)))

    fetch_turned.wait()
    for s in range(8):
        for h in range(2):
            if s >= 4 and h == 0:
                continue
            block = dot(turned_ref[s], grads[:, h * half : (h + 1) * half])
            for r in range(4):
                tap = tap_of(s, 4 * h + r)
                if tap is not None:
                    part_ref[:, tap * c_out : (tap + 1) * c_out] = block[:, r * c_out : (r + 1) * c_out]

    row, col = line((quad, 2 * half), 0), line((quad, 2 * half), 1)
    kept = jnp.where(row // group == col % half // c_out, head_sum[...], 0.0)
    sums = [bias_sum[...]]
    for f in range(FIELDS):
        sums.append(jnp.sum(jnp.where(row % FIELDS == f, kept, 0.0), axis=0, keepdims=True))
    tail = 2 * [sum(x[:, g * c_out : (g + 1) * c_out] for g in range(8)) for x in sums]
    place = line((c_in, c_out), 0) % owner_rows
    for b in range(-(-len(tail) // owner_rows)):
        fill = jnp.zeros((c_in, c_out), jnp.float32)
        for i, value in enumerate(tail[b * owner_rows : (b + 1) * owner_rows]):
            fill = jnp.where(place == i, value, fill)
        part_ref[:, (TAPS + b) * c_out : (TAPS + b + 1) * c_out] = fill


def reduce_kernel(
    c_out, scale, part_ref, out_ref, got, outgoing, landed, send_pair, recv_pair, send_far, recv_far
):
    peers, _, rows, width = part_ref.shape
    me = lax.axis_index("domain")
    side = lax.rem(me, 2)
    home = me // 2
    partner = me + 1 - 2 * side
    edge = TAPS * c_out

    barrier = pltpu.get_barrier_semaphore()
    pl.semaphore_signal(
        barrier, inc=1, device_id={"domain": partner}, device_id_type=pl.DeviceIdType.MESH
    )

    @pl.loop(1, peers)
    def _(step):
        pl.semaphore_signal(
            barrier,
            inc=1,
            device_id={"domain": 2 * lax.rem(home + step, peers) + side},
            device_id_type=pl.DeviceIdType.MESH,
        )

    pl.semaphore_wait(barrier, peers)

    def near(block):
        return pltpu.make_async_remote_copy(
            src_ref=part_ref.at[block, 1 - side],
            dst_ref=got.at[block],
            send_sem=send_pair.at[block],
            recv_sem=recv_pair.at[block],
            device_id={"domain": partner},
            device_id_type=pl.DeviceIdType.MESH,
        )

    def far(block, slot):
        return pltpu.make_async_remote_copy(
            src_ref=outgoing.at[block],
            dst_ref=landed.at[slot],
            send_sem=send_far.at[block],
            recv_sem=recv_far.at[slot],
            device_id={"domain": 2 * block + side},
            device_id_type=pl.DeviceIdType.MESH,
        )

    @pl.loop(1, peers + 1)
    def _(step):
        near(lax.rem(home + step, peers)).start()

    spot = line((rows, width), 0) + (line((rows, width), 1) - edge) // c_out * rows
    in_tail = line((rows, width), 1) >= edge
    low = in_tail & (spot >= FIELDS + 1)

    def pair_sum(block):
        near(block).wait_recv()
        both = part_ref[block, side] + got[block]
        top = both.astype(jnp.bfloat16).astype(jnp.float32)
        return jnp.where(low, both - top, jnp.where(in_tail, top, both))

    @pl.loop(1, peers)
    def _(step):
        block = lax.rem(home + step, peers)
        outgoing[block] = pair_sum(block).astype(jnp.bfloat16)
        far(block, home).start()

    out_ref[...] = pair_sum(home)

    @pl.loop(1, peers)
    def _(step):
        source = lax.rem(home + peers - step, peers)
        far(source, source).wait_recv()
        out_ref[...] += landed[source].astype(jnp.float32)

    out_ref[...] *= scale

    @pl.loop(1, peers)
    def _(step):
        block = lax.rem(home + step, peers)
        near(block).wait_send()
        far(block, home).wait_send()

    near(home).wait_send()


LIMIT = pltpu.CompilerParams(vmem_limit_bytes=22 * 1024 * 1024)


def add_up(part, c_out, owners, scale):
    rows, width = part.shape[0] // owners, part.shape[1]
    peers = owners // 2
    return pl.pallas_call(
        functools.partial(reduce_kernel, c_out, scale),
        out_shape=jax.ShapeDtypeStruct((rows, width), jnp.float32),
        in_specs=[pl.BlockSpec(memory_space=pltpu.VMEM)],
        out_specs=pl.BlockSpec(memory_space=pltpu.VMEM),
        scratch_shapes=[
            pltpu.VMEM((peers, rows, width), jnp.float32),
            pltpu.VMEM((peers, rows, width), jnp.bfloat16),
            pltpu.VMEM((peers, rows, width), jnp.bfloat16),
            pltpu.SemaphoreType.DMA((peers,)),
            pltpu.SemaphoreType.DMA((peers,)),
            pltpu.SemaphoreType.DMA((peers,)),
            pltpu.SemaphoreType.DMA((peers,)),
        ],
        compiler_params=pltpu.CompilerParams(
            collective_id=0, has_side_effects=True, vmem_limit_bytes=22 * 1024 * 1024
        ),
    )(part.reshape(peers, 2, rows, width))


def forward(patches, conv_weight, conv_bias):
    slots, _, c_in = patches.shape
    c_out = conv_weight.shape[2]
    return pl.pallas_call(
        forward_kernel,
        out_shape=(
            pltpu.HBM((slots * COARSE, 8 * c_out), jnp.float32),
            pltpu.HBM((8, c_in, slots * COARSE), jnp.bfloat16),
        ),
        out_specs=(pl.BlockSpec(memory_space=pltpu.HBM),) * 2,
        scratch_shapes=[
            pltpu.VMEM((slots * COARSE, 8 * c_out), jnp.float32),
            pltpu.VMEM((8, c_in, slots * COARSE), jnp.bfloat16),
            pltpu.VMEM((slots * CELLS_UP, c_in), jnp.bfloat16),
            pltpu.VMEM((8 * c_in, 8 * c_out), jnp.bfloat16),
            pltpu.VMEM((16 * COARSE, 2 * CELLS_UP), jnp.bfloat16),
            pltpu.VMEM((2 * CELLS_UP, 16 * COARSE), jnp.bfloat16),
            pltpu.SemaphoreType.DMA((slots // 2,)),
            pltpu.SemaphoreType.DMA((slots // 2,)),
        ],
        compiler_params=LIMIT,
        cost_estimate=pl.CostEstimate(
            flops=8 * slots * COARSE * TAPS * c_in * c_out,
            bytes_accessed=10 * 1024 * 1024,
            transcendentals=0,
        ),
    )(patches, conv_weight.transpose(1, 0, 2), jnp.tile(conv_bias[None, :], (1, 8)))


def backward(hidden, turned, work_cot, head_weight, owner_rows):
    slots = work_cot.shape[0]
    c_in = turned.shape[1]
    c_out = head_weight.shape[0]
    group = slots * FIELDS
    blocks = TAPS + -(-2 * (FIELDS + 1) // owner_rows)
    return pl.pallas_call(
        functools.partial(backward_kernel, owner_rows),
        out_shape=jax.ShapeDtypeStruct((c_in, blocks * c_out), jnp.float32),
        in_specs=[pl.BlockSpec(memory_space=pltpu.HBM)] * 2
        + [pl.BlockSpec(memory_space=pltpu.VMEM)] * 2,
        scratch_shapes=[
            pltpu.VMEM((slots * COARSE, 8 * c_out), jnp.float32),
            pltpu.VMEM((8, c_in, slots * COARSE), jnp.bfloat16),
            pltpu.VMEM((slots * COARSE, 8 * c_out), jnp.bfloat16),
            pltpu.VMEM((COARSE, 8 * group), jnp.bfloat16),
            pltpu.VMEM((12 * group, 4 * c_out), jnp.bfloat16),
            pltpu.VMEM((4 * group, 8 * c_out), jnp.float32),
            pltpu.VMEM((1, 8 * c_out), jnp.float32),
            pltpu.SemaphoreType.DMA((slots // 2,)),
            pltpu.SemaphoreType.DMA,
        ],
        compiler_params=pltpu.CompilerParams(vmem_limit_bytes=61 * 1024 * 1024),
        cost_estimate=pl.CostEstimate(
            flops=8 * slots * COARSE * TAPS * c_in * c_out,
            bytes_accessed=8 * 1024 * 1024,
            transcendentals=slots * FINE * c_out,
        ),
    )(hidden, turned, work_cot.reshape(group, FINE), jnp.tile(head_weight.T, (1, 4)))


def on_device(patches, destination, cotangent, conv_weight, conv_bias, head_weight):
    owners = lax.axis_size("domain")
    own_rows = patches.shape[0]
    train_rows = cotangent.shape[0]
    c_in, _, c_out = conv_weight.shape
    per_pair = (train_rows + owners - 1) // owners
    slot_total = owners * per_pair
    exchange = functools.partial(
        lax.all_to_all, axis_name="domain", split_axis=0, concat_axis=0, tiled=True
    )

    trainer_ids = jnp.arange(owners, dtype=jnp.int32)
    hits = (destination[:, None] == trainer_ids[None, :]).astype(jnp.int32)
    incoming = exchange(jnp.sum(hits, axis=0))
    earlier = jnp.arange(own_rows)[:, None] > jnp.arange(own_rows)[None, :]
    local_rank = jnp.sum(
        (earlier & (destination[:, None] == destination[None, :])).astype(jnp.int32), axis=1
    )
    before = trainer_ids[:, None] > trainer_ids[None, :]
    starts_in = jnp.sum(jnp.where(before, incoming[None, :], 0), axis=1)
    slot_rank = jnp.arange(per_pair, dtype=jnp.int32)
    slot_place = (starts_in[:, None] + slot_rank[None, :]).reshape(slot_total)
    outgoing = cotangent[jnp.minimum(slot_place, train_rows - 1)]
    patches, outgoing = lax.optimization_barrier((patches, outgoing))
    arrived = exchange(outgoing.reshape(owners, per_pair, FIELDS, FINE))
    hidden, turned = forward(patches, conv_weight, conv_bias)
    arrived = arrived.reshape(slot_total, FIELDS, FINE)
    work_cot = arrived[destination * per_pair + local_rank]

    rows = c_in // owners
    part = backward(hidden, turned, work_cot, head_weight, rows)
    scale = float((owners * own_rows * COARSE) ** (-0.5))
    sums = add_up(part, c_out, owners, scale)
    conv = sums[:, : TAPS * c_out].reshape(rows, TAPS, c_out)
    tail = sums[:, TAPS * c_out :].reshape(rows, -1, c_out).transpose(1, 0, 2).reshape(-1, c_out)
    small = tail[: FIELDS + 1] + tail[FIELDS + 1 : 2 * (FIELDS + 1)]
    return conv, small[0], small[1:].T


def solution(mesh):
    placed = (
        P(("groups", "domain"), None, None),
        P(("groups", "domain")),
        P(("groups", "domain"), None, None),
        P(),
        P(),
        P(),
    )
    return jax.shard_map(
        on_device,
        mesh=mesh,
        in_specs=placed,
        out_specs=(P(("groups", "domain"), None, None), P("groups"), P("groups", None)),
        check_vma=False,
    )
```
